32 devices in a mesh: replica: 4 (over y, core), tensor: 8 (over z, x).
Axes of the slice: x: 2, y: 2, z: 4, core: 2. Of those that a mesh axis runs over, the one named last changes fastest.
Arguments:
- tokens: bfloat16 [4, 2048, 8192], P('replica', None, 'tensor'), may hold values from -6 to 6
- kv_grad: bfloat16 [4, 2048, 1024], P('replica', None, 'tensor'), may hold values from -6 to 6
- weights: float32 [4, 8192, 1024], P('replica', 'tensor'), may hold values from -0.0625 to 0.0625
- first_moment: bfloat16 [4, 8192, 1024], P('replica', 'tensor'), may hold values from -240 to 240
- second_moment: bfloat16 [4, 8192, 1024], P('replica', 'tensor'), may hold values from 300 to 5984
- exponent: int32 [8], replicated, may hold values from 0 to 1, as said below
Outputs:
- new_weights: float32 [4, 8192, 1024], P('replica', 'tensor')
- new_first: bfloat16 [4, 8192, 1024], P('replica', 'tensor')
- new_second: bfloat16 [4, 8192, 1024], P('replica', 'tensor')
- input_grad: bfloat16 [4, 2048, 8192], P('replica', None, 'tensor')
The draws below stay inside these ranges and needn't reach their ends.
Inputs may be any that keep to these rules, and one draw needn't show every extreme that they name: One integer per column bucket; the gossip partner of bucket g lies 2 ** exponent[g] replicas away; some bucket takes 0 and some bucket takes the largest allowed value.
All inputs are finite; a program needn't handle non-finite values.
Results may differ from the reference program's by a relative error of at most 0.0049.
Values may be sent and summed in bfloat16 or wider, within the bound.
A program may use at most 128 MiB of HBM per device.

```python
import math
import jax
import jax.numpy as jnp
from jax import lax

D = 8192
TOK = 2048
KV = 1024
BUCKETS = 8
REPLICAS = 4


def draw_exponent(key, part):
    levels = REPLICAS.bit_length() - 1
    base_values = jax.random.randint(jax.random.fold_in(key, 11), (BUCKETS,), 0, levels, dtype=jnp.int32)
    order = jax.random.permutation(jax.random.fold_in(key, 23), BUCKETS)
    positions = jnp.arange(BUCKETS, dtype=jnp.int32)
    top_spot = order[0].astype(jnp.int32)
    low_spot = order[1].astype(jnp.int32)
    with_top = jnp.where(positions == top_spot, jnp.int32(levels - 1), base_values)
    return jnp.where(positions == low_spot, jnp.int32(0), with_top)


def block_levels(stream_key, shape, split, smallest, largest):
    gain = 1.0
    for axis_at, parts in split:
        draws = jax.random.uniform(jax.random.fold_in(jax.random.fold_in(stream_key, 6), axis_at), (parts,), jnp.float32, smallest / len(split), largest / len(split))
        gain = gain * jnp.repeat(jnp.exp(draws), shape[axis_at] // parts).reshape((-1,) + (1,) * (len(shape) - 1 - axis_at))
    return gain


def gaussian(own_key, dims, width, bound, shards=(), held_as=jnp.bfloat16):
    result = jax.random.normal(own_key, dims, jnp.float32) * width
    if len(shards) > 0:
        result = block_levels(own_key, dims, shards, -0.22, 0.18) * result
    return jnp.clip(result, min=-bound, max=bound).astype(held_as)


def setup_inputs(seed: int = 0) -> dict:
    key_of = jax.random.split(jax.random.key(seed), 7)
    tokens = gaussian(key_of[0], (REPLICAS, TOK, D), 1.0, 6.0, ((0, 4), (2, 8)))
    kv_grad = gaussian(key_of[1], (REPLICAS, TOK, KV), 1.0, 6.0, ((0, 4), (2, 8)))
    weights = gaussian(key_of[2], (REPLICAS, D, KV), D ** -0.5, 0.0625, ((0, 4), (1, 8)), jnp.float32)
    first_moment = gaussian(key_of[3], (REPLICAS, D, KV), 40.0, 240.0, ((0, 4), (1, 8)))
    second_moment = jnp.clip(jnp.exp(math.log(5984.0) - 2.993062 * jax.random.uniform(key_of[4], (REPLICAS, D, KV), jnp.float32) ** block_levels(key_of[4], (REPLICAS, D, KV), ((0, 4), (1, 8)), -0.2, 0.2)), 300.0, 5984.0).astype(jnp.bfloat16)
    exponent = draw_exponent(jax.random.fold_in(key_of[6], 71), 0)
    return {"tokens": tokens, "kv_grad": kv_grad, "weights": weights, "first_moment": first_moment, "second_moment": second_moment, "exponent": exponent}


learn_rate = 0.00015
beta_first = 0.9
beta_second = 0.95
decay_rate = 0.1
epsilon = 1e-08

def replica_grads(inputs):
    acts, cotangent, master = inputs
    grad_here = jnp.dot(acts.T, cotangent, preferred_element_type=jnp.float32)
    master_low = master.astype(jnp.bfloat16)
    back = jnp.dot(cotangent, master_low.T, preferred_element_type=jnp.float32).astype(jnp.bfloat16)
    return (grad_here, back)

def reference(tokens, kv_grad, weights, first_moment, second_moment, exponent):
    grads, input_grad = lax.map(replica_grads, (tokens, kv_grad, weights))
    bucket_count = exponent.shape[0]
    bucket_width = weights.shape[2] // bucket_count
    pieces = []
    for bucket_index in range(bucket_count):
        hop_count = jnp.left_shift(jnp.int32(1), exponent[bucket_index].astype(jnp.int32))
        sources = (jnp.arange(REPLICAS, dtype=jnp.int32) - hop_count) % REPLICAS
        columns = weights[:, :, bucket_index * bucket_width:(bucket_index + 1) * bucket_width]
        pieces.append(jnp.take(columns, sources.astype(jnp.int32), axis=0))
    partner = jnp.concatenate(pieces, axis=2)
    averaged = 0.5 * (weights + partner)
    first = beta_first * first_moment.astype(jnp.float32) + (1.0 - beta_first) * grads
    second = beta_second * second_moment.astype(jnp.float32) + (1.0 - beta_second) * grads * grads
    direction = first / (jnp.sqrt(second) + epsilon)
    new_weights = averaged - learn_rate * (direction + decay_rate * averaged)
    return (new_weights, first.astype(jnp.bfloat16), second.astype(jnp.bfloat16), input_grad)
```

```python
import jax
import jax.numpy as jnp
from jax import lax
from jax.experimental import pallas as pl
from jax.experimental.pallas import tpu as pltpu
from jax.sharding import PartitionSpec as P

learn_rate = 0.00015
beta_first = 0.9
beta_second = 0.95
decay_rate = 0.1
epsilon = 1e-08


def for_sending(array):
    return jax.tree.map(lambda a: a.astype(jnp.bfloat16) if a.dtype == jnp.float32 else a, array)


def from_behind(array, axis, by):
    count = lax.axis_size(axis)
    return lax.ppermute(array, axis, [(i, (i + by) % count) for i in range(count)])


def build_branch(hop_count):

    def fetch_peer(source_array):
        return jax.tree.map(
            lambda part, own: part.astype(own.dtype),
            from_behind(for_sending(source_array), "replica", hop_count),
            source_array,
        )

    return fetch_peer


def bucket_gossip(source_array, exponent, builder):
    levels = lax.axis_size("replica").bit_length() - 1
    branches = [builder(1 << bit_index) for bit_index in range(levels)]
    bucket_count = exponent.shape[0]
    bucket_width = source_array.shape[2] // bucket_count
    pieces = []
    for bucket_index in range(bucket_count):
        columns = source_array[
            :, :, bucket_index * bucket_width : (bucket_index + 1) * bucket_width
        ]
        pieces.append(lax.switch(exponent[bucket_index], branches, columns))
    return jnp.concatenate(pieces, axis=2)


def adam_update(master_part, partner_part, grad_part, first_part, second_part):
    averaged = 0.5 * (master_part + partner_part)
    first = beta_first * first_part.astype(jnp.float32) + (1.0 - beta_first) * grad_part
    second = (
        beta_second * second_part.astype(jnp.float32) + (1.0 - beta_second) * grad_part * grad_part
    )
    direction = first / (jnp.sqrt(second) + epsilon)
    new_weights = averaged - learn_rate * (direction + decay_rate * averaged)
    return (new_weights, first.astype(jnp.bfloat16), second.astype(jnp.bfloat16))


def on_device(tokens, kv_grad, weights, first_moment, second_moment, exponent):
    acts = tokens[0]
    local_cols = kv_grad[0]
    master = weights[0]
    master_low = master.astype(jnp.bfloat16)
    whole_grad = lax.all_gather(local_cols, "tensor", axis=1, tiled=True)
    grad_here = jnp.dot(acts.T, whole_grad, preferred_element_type=jnp.float32)
    back = jnp.dot(whole_grad, master_low.T, preferred_element_type=jnp.float32)
    partner = bucket_gossip(weights, exponent, build_branch)
    new_weights, new_first, new_second = adam_update(
        master, partner[0], grad_here, first_moment[0], second_moment[0]
    )
    return (new_weights[None], new_first[None], new_second[None], back.astype(jnp.bfloat16)[None])


CHUNKS = 4
PLANES = 4
BLOCKS = 8
TILE = 256


def fused_kernel(
    exponent, tokens, kv_grad, weights, first_moment, second_moment,
    new_weights, new_first, new_second, input_grad,
    gathered, tok, tok_t, master, low, other, outgoing, incoming, first_in, second_in, grad_acc, back_acc,
    up_sem, down_sem, across_sem, block_sem, core_send, core_recv, peer_send, peer_recv,
    own_sem, master_sem, tok_sem, first_sem, second_sem,
):
    replica = lax.axis_index("replica")
    place = lax.axis_index("tensor")
    core = lax.rem(replica, 2)
    z = lax.div(place, 2)
    x = lax.rem(place, 2)
    rows_of = tokens.shape[0] // CHUNKS
    width = kv_grad.shape[1]
    depth = weights.shape[0]

    above = {"tensor": lax.rem(place + 2, 2 * PLANES)}
    below = {"tensor": lax.rem(place + 2 * PLANES - 2, 2 * PLANES)}
    across = {"tensor": place + 1 - 2 * x}
    twin = {"replica": replica + 1 - 2 * core}
    peer = {"replica": lax.rem(replica + 2, 4)}
    has_above = z < PLANES - 1
    has_below = z > 0

    order = [
        z,
        jnp.where(z == 0, 1, z - 1),
        jnp.where(z == 0, 2, jnp.where(z == 1, 2, jnp.where(z == 2, 3, 1))),
        jnp.where(z < 2, 3, 0),
    ]

    def rows(c):
        return pl.ds(c * rows_of, rows_of)

    def columns(g):
        return pl.ds(pl.multiple_of(g * width, width), width)

    def hop(plane, c, target, send_sem):
        block = plane * 2 + x
        piece = gathered.at[block, rows(c)]
        return pltpu.make_async_remote_copy(
            src_ref=piece, dst_ref=piece, send_sem=send_sem.at[plane, c], recv_sem=block_sem.at[block, c],
            device_id=target, device_id_type=pl.DeviceIdType.MESH,
        )

    def arrived(block, c):
        piece = gathered.at[block, rows(c)]
        pltpu.make_async_remote_copy(
            src_ref=piece, dst_ref=piece, send_sem=across_sem.at[0, 0], recv_sem=block_sem.at[block, c],
            device_id=across, device_id_type=pl.DeviceIdType.MESH,
        ).wait_recv()

    def to_twin(g):
        return pltpu.make_async_remote_copy(
            src_ref=low.at[g], dst_ref=other.at[g], send_sem=core_send.at[g], recv_sem=core_recv.at[g],
            device_id=twin, device_id_type=pl.DeviceIdType.MESH,
        )

    def to_peer(g):
        return pltpu.make_async_remote_copy(
            src_ref=outgoing.at[g], dst_ref=incoming.at[g], send_sem=peer_send.at[g], recv_sem=peer_recv.at[g],
            device_id=peer, device_id_type=pl.DeviceIdType.MESH,
        )

    load_own = pltpu.make_async_copy(kv_grad, gathered.at[place], own_sem)
    load_own.start()

    def load_master(g):
        return pltpu.make_async_copy(weights.at[:, columns(g)], master.at[:, columns(g)], master_sem.at[g])

    buckets = [order[i // 2] * 2 + i % 2 for i in range(BLOCKS)]
    for g in buckets:
        load_master(g).start()
    load_tok = [pltpu.make_async_copy(tokens.at[rows(c)], tok.at[rows(c)], tok_sem.at[c]) for c in range(CHUNKS)]
    for copy in load_tok:
        copy.start()
    load_first = pltpu.make_async_copy(first_moment, first_in, first_sem)
    load_second = pltpu.make_async_copy(second_moment, second_in, second_sem)
    load_first.start()
    load_second.start()

    barrier = pltpu.get_barrier_semaphore()
    for target in (across, twin, peer):
        pl.semaphore_signal(barrier, inc=1, device_id=target, device_id_type=pl.DeviceIdType.MESH)

    @pl.when(has_above)
    def _():
        pl.semaphore_signal(barrier, inc=1, device_id=above, device_id_type=pl.DeviceIdType.MESH)

    @pl.when(has_below)
    def _():
        pl.semaphore_signal(barrier, inc=1, device_id=below, device_id_type=pl.DeviceIdType.MESH)

    pl.semaphore_wait(barrier, 3 + has_above.astype(jnp.int32) + has_below.astype(jnp.int32))

    load_own.wait()
    for c in range(CHUNKS):
        @pl.when(has_above)
        def _():
            hop(z, c, above, up_sem).start()

        @pl.when(has_below)
        def _():
            hop(z, c, below, down_sem).start()

        hop(z, c, across, across_sem).start()

    for g in buckets:
        load_master(g).wait()
        low[g] = master[:, columns(g)].astype(jnp.bfloat16)
        to_twin(g).start()

        @pl.when(core == 1)
        def _():
            outgoing[g] = low[g]
            to_peer(g).start()

    for g in buckets:
        to_twin(g).wait_recv()

        @pl.when(core == 0)
        def _():
            near = jnp.full((16, width), exponent[g], jnp.int32).astype(jnp.float32)
            near = jnp.where(near == 0.0, 1.0, 0.0)[0:1]
            outgoing[g] = (
                other[g].astype(jnp.float32) * near + low[g].astype(jnp.float32) * (1.0 - near)
            ).astype(jnp.bfloat16)
            to_peer(g).start()

    for c in range(CHUNKS):
        load_tok[c].wait()
        tok_t[:, rows(c)] = tok[rows(c), :].T

    def multiply(plane, c, last):
        start = pl.multiple_of(c * rows_of, rows_of)
        part = pl.ds(start, rows_of)

        def piece():
            return jnp.concatenate([gathered[plane * 2, part], gathered[plane * 2 + 1, part]], axis=1)

        @pl.loop(0, depth // TILE)
        def _(i):
            tile = pl.ds(pl.multiple_of(i * TILE, TILE), TILE)
            term = jnp.dot(tok_t[tile, part], piece(), preferred_element_type=jnp.float32)
            grad_acc[tile, :] = jnp.where(c == 0, term, grad_acc[tile, :] + term) if not isinstance(c, int) else (
                term if c == 0 else grad_acc[tile, :] + term
            )

        @pl.loop(0, depth // TILE)
        def _(i):
            tile = pl.ds(pl.multiple_of(i * TILE, TILE), TILE)
            weight = jnp.concatenate([low[plane * 2, tile], low[plane * 2 + 1, tile]], axis=1)
            term = lax.dot_general(piece(), weight, (((1,), (1,)), ((), ())), preferred_element_type=jnp.float32)
            if last == "first":
                back_acc[part, tile] = term
            elif last == "middle":
                back_acc[part, tile] += term
            else:
                input_grad[part, tile] = (back_acc[part, tile] + term).astype(jnp.bfloat16)

    def update(plane):
        for side in range(2):
            g = plane * 2 + side
            to_peer(g).wait_recv()
            near = jnp.full((16, width), exponent[g], jnp.int32).astype(jnp.float32)
            near = jnp.where(near == 0.0, 1.0, 0.0)[0:1] * core.astype(jnp.float32)

            @pl.loop(0, depth // TILE)
            def _(i):
                tile = pl.ds(pl.multiple_of(i * TILE, TILE), TILE)
                at = columns(g)
                grad = grad_acc[tile, side * width:(side + 1) * width]
                partner = (
                    other[g, tile].astype(jnp.float32) * near
                    + incoming[g, tile].astype(jnp.float32) * (1.0 - near)
                )
                averaged = 0.5 * (master[tile, at] + partner)
                first = beta_first * first_in[tile, at].astype(jnp.float32) + (1.0 - beta_first) * grad
                second = (
                    beta_second * second_in[tile, at].astype(jnp.float32)
                    + (1.0 - beta_second) * grad * grad
                )
                direction = first / (jnp.sqrt(second) + epsilon)
                new_weights[tile, at] = averaged - learn_rate * (direction + decay_rate * averaged)
                new_first[tile, at] = first.astype(jnp.bfloat16)
                new_second[tile, at] = second.astype(jnp.bfloat16)

    for phase in range(1, PLANES + 1):
        for c in range(CHUNKS):
            if phase < PLANES:
                @pl.when(z - phase >= 0)
                def _():
                    plane = lax.rem(z - phase + PLANES, PLANES)
                    arrived(plane * 2 + x, c)

                    @pl.when(has_above)
                    def _():
                        hop(plane, c, above, up_sem).start()

                @pl.when(z + phase < PLANES)
                def _():
                    plane = lax.rem(z + phase, PLANES)
                    arrived(plane * 2 + x, c)

                    @pl.when(has_below)
                    def _():
                        hop(plane, c, below, down_sem).start()

                hop(order[phase], c, across, across_sem).start()
            plane = order[phase - 1]
            arrived(plane * 2 + 1 - x, c)
            multiply(plane, c, "first" if phase == 1 else "middle" if phase < PLANES else "last")
        if phase == 1:
            load_first.wait()
            load_second.wait()
        update(plane)

    for c in range(CHUNKS):
        for plane in range(PLANES):
            hop(plane, c, across, across_sem).wait_send()

            @pl.when(jnp.logical_and(has_above, plane <= z))
            def _():
                hop(plane, c, above, up_sem).wait_send()

            @pl.when(jnp.logical_and(has_below, plane >= z))
            def _():
                hop(plane, c, below, down_sem).wait_send()

    for g in range(BLOCKS):
        to_twin(g).wait_send()
        to_peer(g).wait_send()


def on_device_fused(tokens, kv_grad, weights, first_moment, second_moment, exponent):
    tok, width, depth = tokens.shape[1], kv_grad.shape[2], weights.shape[1]
    bf16, f32 = jnp.bfloat16, jnp.float32
    wide = width * BLOCKS
    any_space = pl.BlockSpec(memory_space=pl.ANY)
    outs = pl.pallas_call(
        fused_kernel,
        out_shape=(
            pltpu.VMEM((depth, wide), f32),
            pltpu.VMEM((depth, wide), bf16),
            pltpu.VMEM((depth, wide), bf16),
            pltpu.VMEM((tok, depth), bf16),
        ),
        in_specs=[pl.BlockSpec(memory_space=pltpu.SMEM)] + [any_space] * 5,
        out_specs=[pl.BlockSpec(memory_space=pltpu.VMEM)] * 4,
        scratch_shapes=[
            pltpu.VMEM((BLOCKS, tok, width), bf16),
            pltpu.VMEM((tok, depth), bf16),
            pltpu.VMEM((depth, tok), bf16),
            pltpu.VMEM((depth, wide), f32),
            pltpu.VMEM((BLOCKS, depth, width), bf16),
            pltpu.VMEM((BLOCKS, depth, width), bf16),
            pltpu.VMEM((BLOCKS, depth, width), bf16),
            pltpu.VMEM((BLOCKS, depth, width), bf16),
            pltpu.VMEM((depth, wide), bf16),
            pltpu.VMEM((depth, wide), bf16),
            pltpu.VMEM((depth, 2 * width), f32),
            pltpu.VMEM((tok, depth), f32),
            pltpu.SemaphoreType.DMA((PLANES, CHUNKS)),
            pltpu.SemaphoreType.DMA((PLANES, CHUNKS)),
            pltpu.SemaphoreType.DMA((PLANES, CHUNKS)),
            pltpu.SemaphoreType.DMA((BLOCKS, CHUNKS)),
            pltpu.SemaphoreType.DMA((BLOCKS,)),
            pltpu.SemaphoreType.DMA((BLOCKS,)),
            pltpu.SemaphoreType.DMA((BLOCKS,)),
            pltpu.SemaphoreType.DMA((BLOCKS,)),
            pltpu.SemaphoreType.DMA,
            pltpu.SemaphoreType.DMA((BLOCKS,)),
            pltpu.SemaphoreType.DMA((CHUNKS,)),
            pltpu.SemaphoreType.DMA,
            pltpu.SemaphoreType.DMA,
        ],
        compiler_params=pltpu.CompilerParams(
            collective_id=0, has_side_effects=True, vmem_limit_bytes=46 << 20
        ),
    )(exponent, tokens[0], kv_grad[0], weights[0], first_moment[0], second_moment[0])
    return tuple(out[None] for out in outs)


def solution(mesh):
    small = mesh.shape["replica"] == 4 and mesh.shape["tensor"] == BLOCKS
    placed = (
        P("replica", None, "tensor"),
        P("replica", None, "tensor"),
        P("replica", "tensor", None),
        P("replica", "tensor", None),
        P("replica", "tensor", None),
        P(),
    )
    return jax.shard_map(
        on_device_fused if small else on_device,
        mesh=mesh,
        in_specs=placed,
        out_specs=(
            P("replica", "tensor", None),
            P("replica", "tensor", None),
            P("replica", "tensor", None),
            P("replica", None, "tensor"),
        ),
        check_vma=False,
    )
```

```python
import jax
import jax.numpy as jnp
from jax import lax
from jax.experimental import pallas as pl
from jax.experimental.pallas import tpu as pltpu
from jax.sharding import PartitionSpec as P

learn_rate = 0.00015
beta_first = 0.9
beta_second = 0.95
decay_rate = 0.1
epsilon = 1e-08


def for_sending(array):
    return jax.tree.map(lambda a: a.astype(jnp.bfloat16) if a.dtype == jnp.float32 else a, array)


def from_behind(array, axis, by):
    count = lax.axis_size(axis)
    return lax.ppermute(array, axis, [(i, (i + by) % count) for i in range(count)])


def build_branch(hop_count):

    def fetch_peer(source_array):
        return jax.tree.map(
            lambda part, own: part.astype(own.dtype),
            from_behind(for_sending(source_array), "replica", hop_count),
            source_array,
        )

    return fetch_peer


def bucket_gossip(source_array, exponent, builder):
    levels = lax.axis_size("replica").bit_length() - 1
    branches = [builder(1 << bit_index) for bit_index in range(levels)]
    bucket_count = exponent.shape[0]
    bucket_width = source_array.shape[2] // bucket_count
    pieces = []
    for bucket_index in range(bucket_count):
        columns = source_array[
            :, :, bucket_index * bucket_width : (bucket_index + 1) * bucket_width
        ]
        pieces.append(lax.switch(exponent[bucket_index], branches, columns))
    return jnp.concatenate(pieces, axis=2)


def adam_update(master_part, partner_part, grad_part, first_part, second_part):
    averaged = 0.5 * (master_part + partner_part)
    first = beta_first * first_part.astype(jnp.float32) + (1.0 - beta_first) * grad_part
    second = (
        beta_second * second_part.astype(jnp.float32) + (1.0 - beta_second) * grad_part * grad_part
    )
    direction = first / (jnp.sqrt(second) + epsilon)
    new_weights = averaged - learn_rate * (direction + decay_rate * averaged)
    return (new_weights, first.astype(jnp.bfloat16), second.astype(jnp.bfloat16))


def on_device(tokens, kv_grad, weights, first_moment, second_moment, exponent):
    acts = tokens[0]
    local_cols = kv_grad[0]
    master = weights[0]
    master_low = master.astype(jnp.bfloat16)
    whole_grad = lax.all_gather(local_cols, "tensor", axis=1, tiled=True)
    grad_here = jnp.dot(acts.T, whole_grad, preferred_element_type=jnp.float32)
    back = jnp.dot(whole_grad, master_low.T, preferred_element_type=jnp.float32)
    partner = bucket_gossip(weights, exponent, build_branch)
    new_weights, new_first, new_second = adam_update(
        master, partner[0], grad_here, first_moment[0], second_moment[0]
    )
    return (new_weights[None], new_first[None], new_second[None], back.astype(jnp.bfloat16)[None])


CHUNKS = 4
PLANES = 4
BLOCKS = 8
TILE = 256


HALF = CHUNKS // 2


def plane_order(z):
    return [
        z,
        jnp.where(z == 0, 1, jnp.where(z == 1, 0, jnp.where(z == 2, 3, 2))),
        jnp.where(z == 0, 2, jnp.where(z == 1, 2, 1)),
        jnp.where(z < 2, 3, 0),
    ]


def adam_tile(averaged, grad, first_part, second_part):
    first = beta_first * first_part.astype(jnp.float32) + (1.0 - beta_first) * grad
    second = (
        beta_second * second_part.astype(jnp.float32) + (1.0 - beta_second) * grad * grad
    )
    direction = first / (jnp.sqrt(second) + epsilon)
    new_weights = averaged - learn_rate * (direction + decay_rate * averaged)
    return (new_weights, first.astype(jnp.bfloat16), second.astype(jnp.bfloat16))


def fused_kernel(
    exponent, tokens, kv_grad, weights, first_moment, second_moment,
    master, first_in, second_in, input_grad, grad_acc,
    gathered, tok, tok_t, low, other, outgoing, incoming, back_acc,
    up_sem, down_sem, across_sem, far_sem, block_sem, core_send, core_recv, peer_send, peer_recv,
    own_sem, master_sem, tok_sem, first_sem, second_sem,
):
    replica = lax.axis_index("replica")
    place = lax.axis_index("tensor")
    core = lax.rem(replica, 2)
    z = lax.div(place, 2)
    x = lax.rem(place, 2)
    rows_of = tokens.shape[0] // CHUNKS
    width = kv_grad.shape[1]
    depth = weights.shape[0]

    above = {"tensor": lax.rem(place + 2, 2 * PLANES)}
    below = {"tensor": lax.rem(place + 2 * PLANES - 2, 2 * PLANES)}
    across = {"tensor": place + 1 - 2 * x}
    twin = {"replica": replica + 1 - 2 * core}
    peer = {"replica": lax.rem(replica + 2, 4)}
    has_above = z < PLANES - 1
    has_below = z > 0

    order = plane_order(z)
    at_end = jnp.logical_or(z == 0, z == PLANES - 1)

    def rows(c):
        return pl.ds(c * rows_of, rows_of)

    def columns(g):
        return pl.ds(pl.multiple_of(g * width, width), width)

    def hop(plane, c, target, send_sem):
        block = plane * 2 + x
        piece = gathered.at[block, rows(c)]
        return pltpu.make_async_remote_copy(
            src_ref=piece, dst_ref=piece, send_sem=send_sem.at[plane, c], recv_sem=block_sem.at[block, c],
            device_id=target, device_id_type=pl.DeviceIdType.MESH,
        )

    def far_hop(plane, c, target, way):
        block = plane * 2 + 1 - x
        piece = gathered.at[block, rows(c)]
        return pltpu.make_async_remote_copy(
            src_ref=piece, dst_ref=piece, send_sem=far_sem.at[way, c], recv_sem=block_sem.at[block, c],
            device_id=target, device_id_type=pl.DeviceIdType.MESH,
        )

    def arrived(block, c):
        piece = gathered.at[block, rows(c)]
        pltpu.make_async_remote_copy(
            src_ref=piece, dst_ref=piece, send_sem=across_sem.at[0, 0], recv_sem=block_sem.at[block, c],
            device_id=across, device_id_type=pl.DeviceIdType.MESH,
        ).wait_recv()

    def to_twin(g):
        return pltpu.make_async_remote_copy(
            src_ref=low.at[g], dst_ref=other.at[g], send_sem=core_send.at[g], recv_sem=core_recv.at[g],
            device_id=twin, device_id_type=pl.DeviceIdType.MESH,
        )

    def to_peer(i):
        return pltpu.make_async_remote_copy(
            src_ref=outgoing.at[i], dst_ref=incoming.at[i], send_sem=peer_send.at[i], recv_sem=peer_recv.at[i],
            device_id=peer, device_id_type=pl.DeviceIdType.MESH,
        )

    load_own = pltpu.make_async_copy(kv_grad, gathered.at[place], own_sem)
    load_own.start()

    def load_master(g):
        return pltpu.make_async_copy(weights.at[:, columns(g)], master.at[:, columns(g)], master_sem.at[g])

    buckets = [order[i // 2] * 2 + i % 2 for i in range(BLOCKS)]
    for g in buckets:
        load_master(g).start()
    load_tok = [pltpu.make_async_copy(tokens.at[rows(c)], tok.at[rows(c)], tok_sem.at[c]) for c in range(CHUNKS)]
    for copy in load_tok:
        copy.start()
    load_first = pltpu.make_async_copy(first_moment, first_in, first_sem)
    load_second = pltpu.make_async_copy(second_moment, second_in, second_sem)
    load_first.start()
    load_second.start()

    barrier = pltpu.get_barrier_semaphore()
    for target in (across, twin, peer):
        pl.semaphore_signal(barrier, inc=1, device_id=target, device_id_type=pl.DeviceIdType.MESH)

    @pl.when(has_above)
    def _():
        pl.semaphore_signal(barrier, inc=1, device_id=above, device_id_type=pl.DeviceIdType.MESH)

    @pl.when(has_below)
    def _():
        pl.semaphore_signal(barrier, inc=1, device_id=below, device_id_type=pl.DeviceIdType.MESH)

    pl.semaphore_wait(barrier, 3 + has_above.astype(jnp.int32) + has_below.astype(jnp.int32))

    load_own.wait()
    for c in range(CHUNKS):
        @pl.when(has_above)
        def _():
            hop(z, c, above, up_sem).start()

        @pl.when(has_below)
        def _():
            hop(z, c, below, down_sem).start()

        hop(z, c, across, across_sem).start()

    near = [jnp.where(exponent[g] == 0, 1, 0) for g in buckets]
    passed = []
    for i in range(BLOCKS):
        passed.append(near[i] if i == 0 else jnp.maximum(passed[-1], near[i]))

    def mask(flag):
        flags = jnp.full((16, width), flag, jnp.int32)
        return jnp.where(flags == 1, 1.0, 0.0)[0:1]

    def mix(flag, one, zero):
        return one.astype(jnp.float32) * flag + zero.astype(jnp.float32) * (1.0 - flag)

    for i, g in enumerate(buckets):
        load_master(g).wait()
        low[g] = master[:, columns(g)].astype(jnp.bfloat16)
        to_twin(g).start()
        if i > 0:
            @pl.when(core == 1)
            def _():
                outgoing[i - 1] = mix(mask(passed[i - 1]), low[g], low[buckets[i - 1]]).astype(jnp.bfloat16)
                to_peer(i - 1).start()

    for i, g in enumerate(buckets):
        to_twin(g).wait_recv()

        @pl.when(core == 0)
        def _():
            outgoing[i] = mix(mask(near[i]), other[g], low[g]).astype(jnp.bfloat16)
            to_peer(i).start()

    for c in range(CHUNKS):
        load_tok[c].wait()
        tok_t[:, rows(c)] = tok[rows(c), :].T

    def multiply(plane, c, last):
        start = pl.multiple_of(c * rows_of, rows_of)
        part = pl.ds(start, rows_of)

        def piece():
            return jnp.concatenate([gathered[plane * 2, part], gathered[plane * 2 + 1, part]], axis=1)

        @pl.loop(0, depth // TILE)
        def _(i):
            tile = pl.ds(pl.multiple_of(i * TILE, TILE), TILE)
            term = jnp.dot(tok_t[tile, part], piece(), preferred_element_type=jnp.float32)
            grad_acc[tile, :] = jnp.where(c == 0, term, grad_acc[tile, :] + term) if not isinstance(c, int) else (
                term if c == 0 else grad_acc[tile, :] + term
            )

        @pl.loop(0, depth // TILE)
        def _(i):
            tile = pl.ds(pl.multiple_of(i * TILE, TILE), TILE)
            weight = jnp.concatenate([low[plane * 2, tile], low[plane * 2 + 1, tile]], axis=1)
            term = lax.dot_general(piece(), weight, (((1,), (1,)), ((), ())), preferred_element_type=jnp.float32)
            if last == "first":
                back_acc[part, tile] = term
            elif last == "middle":
                back_acc[part, tile] += term
            else:
                input_grad[part, tile] = (back_acc[part, tile] + term).astype(jnp.bfloat16)

    def update(phase):
        for side in range(2):
            i = (phase - 1) * 2 + side
            g = buckets[i]
            if i < BLOCKS - 1:
                to_peer(i).wait_recv()
            else:
                @pl.when(core == 0)
                def _():
                    to_peer(i).wait_recv()

            on_one = core
            own_chip = mask(near[i] * on_one)
            earlier = mask(passed[i] * on_one)

            @pl.loop(0, depth // TILE)
            def _(n):
                tile = pl.ds(pl.multiple_of(n * TILE, TILE), TILE)
                at = columns(g)
                grad = grad_acc[tile, side * width:(side + 1) * width]
                here = incoming[i, tile].astype(jnp.float32)
                if i == BLOCKS - 1:
                    here = jnp.where(mask(on_one) == 1.0, incoming[i - 1, tile].astype(jnp.float32), here)
                elif i > 0:
                    here = mix(earlier, incoming[i - 1, tile], here)
                averaged = 0.5 * (master[tile, at] + mix(own_chip, other[g, tile], here))
                if phase == PLANES:
                    master[tile, at] = averaged
                else:
                    master[tile, at], first_in[tile, at], second_in[tile, at] = adam_tile(
                        averaged, grad, first_in[tile, at], second_in[tile, at]
                    )

    for phase in range(1, PLANES + 1):
        for c in range(CHUNKS):
            if phase < PLANES:
                @pl.when(z - phase >= 0)
                def _():
                    plane = lax.rem(z - phase + PLANES, PLANES)
                    arrived(plane * 2 + x, c)

                    @pl.when(has_above)
                    def _():
                        hop(plane, c, above, up_sem).start()

                @pl.when(z + phase < PLANES)
                def _():
                    plane = lax.rem(z + phase, PLANES)
                    arrived(plane * 2 + x, c)

                    @pl.when(has_below)
                    def _():
                        hop(plane, c, below, down_sem).start()

                if c < HALF or phase == 2:
                    hop(order[phase], c, across, across_sem).start()
                elif phase == 1:
                    @pl.when(at_end)
                    def _():
                        hop(order[phase], c, across, across_sem).start()
            plane = order[phase - 1]
            away = plane * 2 + 1 - x
            if c < HALF or phase < PLANES:
                arrived(away, c)
            else:
                @pl.when(at_end)
                def _():
                    arrived(away, c)
            if c >= HALF and phase < 3:
                turn = (0, PLANES - 1) if phase == 1 else (1, PLANES - 2)

                @pl.when(z == turn[0])
                def _():
                    far_hop(plane, c, above, 0).start()

                @pl.when(z == turn[1])
                def _():
                    far_hop(plane, c, below, 1).start()
            if c >= HALF and phase == 3:
                @pl.when(jnp.logical_not(at_end))
                def _():
                    arrived(order[3] * 2 + 1 - x, c)

                @pl.when(z == 1)
                def _():
                    far_hop(order[3], c, below, 1).start()

                @pl.when(z == 2)
                def _():
                    far_hop(order[3], c, above, 0).start()
            multiply(plane, c, "first" if phase == 1 else "middle" if phase < PLANES else "last")
        if phase == 1:
            load_first.wait()
            load_second.wait()
        update(phase)

    for c in range(CHUNKS):
        for plane in range(PLANES):
            if c < HALF or plane in (0, 2):
                hop(order[plane], c, across, across_sem).wait_send()
            elif plane == 1:
                @pl.when(at_end)
                def _():
                    hop(order[plane], c, across, across_sem).wait_send()

            @pl.when(jnp.logical_and(has_above, plane <= z))
            def _():
                hop(plane, c, above, up_sem).wait_send()

            @pl.when(jnp.logical_and(has_below, plane >= z))
            def _():
                hop(plane, c, below, down_sem).wait_send()

        if c >= HALF:
            @pl.when(has_above)
            def _():
                far_hop(0, c, above, 0).wait_send()

            @pl.when(has_below)
            def _():
                far_hop(PLANES - 1, c, below, 1).wait_send()

    for g in range(BLOCKS):
        to_twin(g).wait_send()
    for i in range(BLOCKS - 1):
        to_peer(i).wait_send()

    @pl.when(core == 0)
    def _():
        to_peer(BLOCKS - 1).wait_send()


def finish_kernel(
    averaged, first_in, second_in, back, grad_acc, new_weights, new_first, new_second, input_grad,
    weights_out, first_out, second_out, pair_sem, back_sem, last_sem,
):
    order = plane_order(lax.div(lax.axis_index("tensor"), 2))
    depth, wide = grad_acc.shape
    rows_of = back.shape[0] // CHUNKS
    half = depth // 2

    def columns(plane):
        return pl.ds(pl.multiple_of(plane * wide, wide), wide)

    copies = []
    for i in range(PLANES - 1):
        at = columns(order[i])
        for k, (source, target) in enumerate(
            ((averaged, new_weights), (first_in, new_first), (second_in, new_second))
        ):
            copies.append(pltpu.make_async_copy(source.at[:, at], target.at[:, at], pair_sem.at[i, k]))
    for c in range(CHUNKS):
        part = pl.ds(c * rows_of, rows_of)
        copies.append(pltpu.make_async_copy(back.at[part], input_grad.at[part], back_sem.at[c]))
    for copy in copies:
        copy.start()
    at = columns(order[PLANES - 1])
    for h in range(2):
        @pl.loop(0, half // 128)
        def _(n):
            tile = pl.ds(pl.multiple_of(h * half + n * 128, 128), 128)
            weights_out[tile], first_out[tile], second_out[tile] = adam_tile(
                averaged[tile, at], grad_acc[tile], first_in[tile, at], second_in[tile, at]
            )

        part = pl.ds(h * half, half)
        for k, (source, target) in enumerate(
            ((weights_out, new_weights), (first_out, new_first), (second_out, new_second))
        ):
            copy = pltpu.make_async_copy(source.at[part], target.at[part, at], last_sem.at[h, k])
            copy.start()
            copies.append(copy)
    for copy in copies:
        copy.wait()


def on_device_fused(tokens, kv_grad, weights, first_moment, second_moment, exponent):
    tok, width, depth = tokens.shape[1], kv_grad.shape[2], weights.shape[1]
    bf16, f32 = jnp.bfloat16, jnp.float32
    wide = width * BLOCKS
    any_space = pl.BlockSpec(memory_space=pl.ANY)
    outs = pl.pallas_call(
        fused_kernel,
        out_shape=(
            pltpu.VMEM((depth, wide), f32),
            pltpu.VMEM((depth, wide), bf16),
            pltpu.VMEM((depth, wide), bf16),
            pltpu.VMEM((tok, depth), bf16),
            pltpu.VMEM((depth, 2 * width), f32),
        ),
        in_specs=[pl.BlockSpec(memory_space=pltpu.SMEM)] + [any_space] * 5,
        out_specs=[pl.BlockSpec(memory_space=pltpu.VMEM)] * 5,
        scratch_shapes=[
            pltpu.VMEM((BLOCKS, tok, width), bf16),
            pltpu.VMEM((tok, depth), bf16),
            pltpu.VMEM((depth, tok), bf16),
            pltpu.VMEM((BLOCKS, depth, width), bf16),
            pltpu.VMEM((BLOCKS, depth, width), bf16),
            pltpu.VMEM((BLOCKS, depth, width), bf16),
            pltpu.VMEM((BLOCKS, depth, width), bf16),
            pltpu.VMEM((tok, depth), f32),
            pltpu.SemaphoreType.DMA((PLANES, CHUNKS)),
            pltpu.SemaphoreType.DMA((PLANES, CHUNKS)),
            pltpu.SemaphoreType.DMA((PLANES, CHUNKS)),
            pltpu.SemaphoreType.DMA((2, CHUNKS)),
            pltpu.SemaphoreType.DMA((BLOCKS, CHUNKS)),
            pltpu.SemaphoreType.DMA((BLOCKS,)),
            pltpu.SemaphoreType.DMA((BLOCKS,)),
            pltpu.SemaphoreType.DMA((BLOCKS,)),
            pltpu.SemaphoreType.DMA((BLOCKS,)),
            pltpu.SemaphoreType.DMA,
            pltpu.SemaphoreType.DMA((BLOCKS,)),
            pltpu.SemaphoreType.DMA((CHUNKS,)),
            pltpu.SemaphoreType.DMA,
            pltpu.SemaphoreType.DMA,
        ],
        compiler_params=pltpu.CompilerParams(
            collective_id=0, has_side_effects=True, vmem_limit_bytes=46 << 20
        ),
    )(exponent, tokens[0], kv_grad[0], weights[0], first_moment[0], second_moment[0])
    results = pl.pallas_call(
        finish_kernel,
        out_shape=(
            jax.ShapeDtypeStruct((depth, wide), f32),
            jax.ShapeDtypeStruct((depth, wide), bf16),
            jax.ShapeDtypeStruct((depth, wide), bf16),
            jax.ShapeDtypeStruct((tok, depth), bf16),
        ),
        in_specs=[pl.BlockSpec(memory_space=pltpu.VMEM)] * 5,
        out_specs=[any_space] * 4,
        scratch_shapes=[
            pltpu.VMEM((depth, 2 * width), f32),
            pltpu.VMEM((depth, 2 * width), bf16),
            pltpu.VMEM((depth, 2 * width), bf16),
            pltpu.SemaphoreType.DMA((PLANES - 1, 3)),
            pltpu.SemaphoreType.DMA((CHUNKS,)),
            pltpu.SemaphoreType.DMA((2, 3)),
        ],
        compiler_params=pltpu.CompilerParams(vmem_limit_bytes=24 << 20),
    )(*outs)
    return tuple(out[None] for out in results)


def solution(mesh):
    small = mesh.shape["replica"] == 4 and mesh.shape["tensor"] == BLOCKS
    placed = (
        P("replica", None, "tensor"),
        P("replica", None, "tensor"),
        P("replica", "tensor", None),
        P("replica", "tensor", None),
        P("replica", "tensor", None),
        P(),
    )
    return jax.shard_map(
        on_device_fused if small else on_device,
        mesh=mesh,
        in_specs=placed,
        out_specs=(
            P("replica", "tensor", None),
            P("replica", "tensor", None),
            P("replica", "tensor", None),
            P("replica", None, "tensor"),
        ),
        check_vma=False,
    )
```

```python
import jax
import jax.numpy as jnp
from jax import lax
from jax.experimental import pallas as pl
from jax.experimental.pallas import tpu as pltpu
from jax.sharding import PartitionSpec as P

learn_rate = 0.00015
beta_first = 0.9
beta_second = 0.95
decay_rate = 0.1
epsilon = 1e-08


def for_sending(array):
    return jax.tree.map(lambda a: a.astype(jnp.bfloat16) if a.dtype == jnp.float32 else a, array)


def from_behind(array, axis, by):
    count = lax.axis_size(axis)
    return lax.ppermute(array, axis, [(i, (i + by) % count) for i in range(count)])


def build_branch(hop_count):

    def fetch_peer(source_array):
        return jax.tree.map(
            lambda part, own: part.astype(own.dtype),
            from_behind(for_sending(source_array), "replica", hop_count),
            source_array,
        )

    return fetch_peer


def bucket_gossip(source_array, exponent, builder):
    levels = lax.axis_size("replica").bit_length() - 1
    branches = [builder(1 << bit_index) for bit_index in range(levels)]
    bucket_count = exponent.shape[0]
    bucket_width = source_array.shape[2] // bucket_count
    pieces = []
    for bucket_index in range(bucket_count):
        columns = source_array[
            :, :, bucket_index * bucket_width : (bucket_index + 1) * bucket_width
        ]
        pieces.append(lax.switch(exponent[bucket_index], branches, columns))
    return jnp.concatenate(pieces, axis=2)


def adam_update(master_part, partner_part, grad_part, first_part, second_part):
    averaged = 0.5 * (master_part + partner_part)
    first = beta_first * first_part.astype(jnp.float32) + (1.0 - beta_first) * grad_part
    second = (
        beta_second * second_part.astype(jnp.float32) + (1.0 - beta_second) * grad_part * grad_part
    )
    direction = first / (jnp.sqrt(second) + epsilon)
    new_weights = averaged - learn_rate * (direction + decay_rate * averaged)
    return (new_weights, first.astype(jnp.bfloat16), second.astype(jnp.bfloat16))


def on_device(tokens, kv_grad, weights, first_moment, second_moment, exponent):
    acts = tokens[0]
    local_cols = kv_grad[0]
    master = weights[0]
    master_low = master.astype(jnp.bfloat16)
    whole_grad = lax.all_gather(local_cols, "tensor", axis=1, tiled=True)
    grad_here = jnp.dot(acts.T, whole_grad, preferred_element_type=jnp.float32)
    back = jnp.dot(whole_grad, master_low.T, preferred_element_type=jnp.float32)
    partner = bucket_gossip(weights, exponent, build_branch)
    new_weights, new_first, new_second = adam_update(
        master, partner[0], grad_here, first_moment[0], second_moment[0]
    )
    return (new_weights[None], new_first[None], new_second[None], back.astype(jnp.bfloat16)[None])


CHUNKS = 4
PLANES = 4
BLOCKS = 8
TILE = 256


HALF = CHUNKS // 2


def plane_order(z):
    return [
        z,
        jnp.where(z == 0, 1, jnp.where(z == 1, 0, jnp.where(z == 2, 3, 2))),
        jnp.where(z == 0, 2, jnp.where(z == 1, 2, 1)),
        jnp.where(z < 2, 3, 0),
    ]


def adam_tile(averaged, grad, first_part, second_part):
    first = beta_first * first_part.astype(jnp.float32) + (1.0 - beta_first) * grad
    second = (
        beta_second * second_part.astype(jnp.float32) + (1.0 - beta_second) * grad * grad
    )
    direction = first / (jnp.sqrt(second) + epsilon)
    new_weights = averaged - learn_rate * (direction + decay_rate * averaged)
    return (new_weights, first.astype(jnp.bfloat16), second.astype(jnp.bfloat16))


def fused_kernel(
    exponent, tokens, kv_grad, weights, first_moment, second_moment,
    master, first_in, second_in, input_grad, grad_acc,
    gathered, tok, tok_t, low, other, outgoing, incoming, back_acc,
    up_sem, down_sem, across_sem, far_sem, block_sem, core_send, core_recv, peer_send, peer_recv,
    own_sem, master_sem, tok_sem, first_sem, second_sem,
):
    replica = lax.axis_index("replica")
    place = lax.axis_index("tensor")
    core = lax.rem(replica, 2)
    z = lax.div(place, 2)
    x = lax.rem(place, 2)
    rows_of = tokens.shape[0] // CHUNKS
    width = kv_grad.shape[1]
    depth = weights.shape[0]

    above = {"tensor": lax.rem(place + 2, 2 * PLANES)}
    below = {"tensor": lax.rem(place + 2 * PLANES - 2, 2 * PLANES)}
    across = {"tensor": place + 1 - 2 * x}
    twin = {"replica": replica + 1 - 2 * core}
    peer = {"replica": lax.rem(replica + 2, 4)}
    has_above = z < PLANES - 1
    has_below = z > 0

    order = plane_order(z)
    at_end = jnp.logical_or(z == 0, z == PLANES - 1)

    def rows(c):
        return pl.ds(c * rows_of, rows_of)

    def columns(g):
        return pl.ds(pl.multiple_of(g * width, width), width)

    def hop(plane, c, target, send_sem):
        block = plane * 2 + x
        piece = gathered.at[block, rows(c)]
        return pltpu.make_async_remote_copy(
            src_ref=piece, dst_ref=piece, send_sem=send_sem.at[plane, c], recv_sem=block_sem.at[block, c],
            device_id=target, device_id_type=pl.DeviceIdType.MESH,
        )

    def far_hop(plane, c, target, way):
        block = plane * 2 + 1 - x
        piece = gathered.at[block, rows(c)]
        return pltpu.make_async_remote_copy(
            src_ref=piece, dst_ref=piece, send_sem=far_sem.at[way, c], recv_sem=block_sem.at[block, c],
            device_id=target, device_id_type=pl.DeviceIdType.MESH,
        )

    def arrived(block, c):
        piece = gathered.at[block, rows(c)]
        pltpu.make_async_remote_copy(
            src_ref=piece, dst_ref=piece, send_sem=across_sem.at[0, 0], recv_sem=block_sem.at[block, c],
            device_id=across, device_id_type=pl.DeviceIdType.MESH,
        ).wait_recv()

    def to_twin(g):
        return pltpu.make_async_remote_copy(
            src_ref=low.at[g], dst_ref=other.at[g], send_sem=core_send.at[g], recv_sem=core_recv.at[g],
            device_id=twin, device_id_type=pl.DeviceIdType.MESH,
        )

    def to_peer(i):
        return pltpu.make_async_remote_copy(
            src_ref=outgoing.at[i], dst_ref=incoming.at[i], send_sem=peer_send.at[i], recv_sem=peer_recv.at[i],
            device_id=peer, device_id_type=pl.DeviceIdType.MESH,
        )

    load_own = pltpu.make_async_copy(kv_grad, gathered.at[place], own_sem)
    load_own.start()

    def load_master(g):
        return pltpu.make_async_copy(weights.at[:, columns(g)], master.at[:, columns(g)], master_sem.at[g])

    buckets = [order[i // 2] * 2 + i % 2 for i in range(BLOCKS)]
    for g in buckets:
        load_master(g).start()
    load_tok = [pltpu.make_async_copy(tokens.at[rows(c)], tok.at[rows(c)], tok_sem.at[c]) for c in range(CHUNKS)]
    load_first = pltpu.make_async_copy(first_moment, first_in, first_sem)
    load_second = pltpu.make_async_copy(second_moment, second_in, second_sem)

    barrier = pltpu.get_barrier_semaphore()
    for target in (across, twin, peer):
        pl.semaphore_signal(barrier, inc=1, device_id=target, device_id_type=pl.DeviceIdType.MESH)

    @pl.when(has_above)
    def _():
        pl.semaphore_signal(barrier, inc=1, device_id=above, device_id_type=pl.DeviceIdType.MESH)

    @pl.when(has_below)
    def _():
        pl.semaphore_signal(barrier, inc=1, device_id=below, device_id_type=pl.DeviceIdType.MESH)

    pl.semaphore_wait(barrier, 3 + has_above.astype(jnp.int32) + has_below.astype(jnp.int32))

    load_own.wait()
    for c in range(CHUNKS):
        @pl.when(has_above)
        def _():
            hop(z, c, above, up_sem).start()

        @pl.when(has_below)
        def _():
            hop(z, c, below, down_sem).start()

        hop(z, c, across, across_sem).start()

    near = [jnp.where(exponent[g] == 0, 1, 0) for g in buckets]
    passed = []
    for i in range(BLOCKS):
        passed.append(near[i] if i == 0 else jnp.maximum(passed[-1], near[i]))

    def mask(flag):
        flags = jnp.full((16, width), flag, jnp.int32)
        return jnp.where(flags == 1, 1.0, 0.0)[0:1]

    def mix(flag, one, zero):
        return one.astype(jnp.float32) * flag + zero.astype(jnp.float32) * (1.0 - flag)

    for i, g in enumerate(buckets):
        load_master(g).wait()
        low[g] = master[:, columns(g)].astype(jnp.bfloat16)
        to_twin(g).start()
        if i > 0:
            @pl.when(core == 1)
            def _():
                outgoing[i - 1] = mix(mask(passed[i - 1]), low[g], low[buckets[i - 1]]).astype(jnp.bfloat16)
                to_peer(i - 1).start()

    for copy in load_tok:
        copy.start()
    load_first.start()
    load_second.start()

    for i, g in enumerate(buckets):
        to_twin(g).wait_recv()

        @pl.when(core == 0)
        def _():
            outgoing[i] = mix(mask(near[i]), other[g], low[g]).astype(jnp.bfloat16)
            to_peer(i).start()

    for c in range(CHUNKS):
        load_tok[c].wait()
        tok_t[:, rows(c)] = tok[rows(c), :].T

    def multiply(plane, c, last):
        start = pl.multiple_of(c * rows_of, rows_of)
        part = pl.ds(start, rows_of)

        def piece():
            return jnp.concatenate([gathered[plane * 2, part], gathered[plane * 2 + 1, part]], axis=1)

        @pl.loop(0, depth // TILE)
        def _(i):
            tile = pl.ds(pl.multiple_of(i * TILE, TILE), TILE)
            term = jnp.dot(tok_t[tile, part], piece(), preferred_element_type=jnp.float32)
            grad_acc[tile, :] = jnp.where(c == 0, term, grad_acc[tile, :] + term) if not isinstance(c, int) else (
                term if c == 0 else grad_acc[tile, :] + term
            )

        @pl.loop(0, depth // TILE)
        def _(i):
            tile = pl.ds(pl.multiple_of(i * TILE, TILE), TILE)
            weight = jnp.concatenate([low[plane * 2, tile], low[plane * 2 + 1, tile]], axis=1)
            term = lax.dot_general(piece(), weight, (((1,), (1,)), ((), ())), preferred_element_type=jnp.float32)
            if last == "first":
                back_acc[part, tile] = term
            elif last == "middle":
                back_acc[part, tile] += term
            else:
                input_grad[part, tile] = (back_acc[part, tile] + term).astype(jnp.bfloat16)

    def update(phase):
        for side in range(2):
            i = (phase - 1) * 2 + side
            g = buckets[i]
            if i < BLOCKS - 1:
                to_peer(i).wait_recv()
            else:
                @pl.when(core == 0)
                def _():
                    to_peer(i).wait_recv()

            on_one = core
            own_chip = mask(near[i] * on_one)
            earlier = mask(passed[i] * on_one)

            @pl.loop(0, depth // TILE)
            def _(n):
                tile = pl.ds(pl.multiple_of(n * TILE, TILE), TILE)
                at = columns(g)
                grad = grad_acc[tile, side * width:(side + 1) * width]
                here = incoming[i, tile].astype(jnp.float32)
                if i == BLOCKS - 1:
                    here = jnp.where(mask(on_one) == 1.0, incoming[i - 1, tile].astype(jnp.float32), here)
                elif i > 0:
                    here = mix(earlier, incoming[i - 1, tile], here)
                averaged = 0.5 * (master[tile, at] + mix(own_chip, other[g, tile], here))
                if phase == PLANES:
                    master[tile, at] = averaged
                else:
                    master[tile, at], first_in[tile, at], second_in[tile, at] = adam_tile(
                        averaged, grad, first_in[tile, at], second_in[tile, at]
                    )

    for phase in range(1, PLANES + 1):
        for c in range(CHUNKS) if phase < PLANES else (0, 2, 1, 3):
            if phase < PLANES:
                @pl.when(z - phase >= 0)
                def _():
                    plane = lax.rem(z - phase + PLANES, PLANES)
                    arrived(plane * 2 + x, c)

                    @pl.when(has_above)
                    def _():
                        hop(plane, c, above, up_sem).start()

                @pl.when(z + phase < PLANES)
                def _():
                    plane = lax.rem(z + phase, PLANES)
                    arrived(plane * 2 + x, c)

                    @pl.when(has_below)
                    def _():
                        hop(plane, c, below, down_sem).start()

                if c < HALF or phase == 2:
                    hop(order[phase], c, across, across_sem).start()
                elif phase == 1:
                    @pl.when(at_end)
                    def _():
                        hop(order[phase], c, across, across_sem).start()
            plane = order[phase - 1]
            away = plane * 2 + 1 - x
            if c < HALF or phase < PLANES:
                arrived(away, c)
            else:
                @pl.when(at_end)
                def _():
                    arrived(away, c)
            if c >= HALF and phase < 3:
                turn = (0, PLANES - 1) if phase == 1 else (1, PLANES - 2)

                @pl.when(z == turn[0])
                def _():
                    far_hop(plane, c, above, 0).start()

                @pl.when(z == turn[1])
                def _():
                    far_hop(plane, c, below, 1).start()
            if c >= HALF and phase == 3:
                @pl.when(jnp.logical_not(at_end))
                def _():
                    arrived(order[3] * 2 + 1 - x, c)

                @pl.when(z == 1)
                def _():
                    far_hop(order[3], c, below, 1).start()

                @pl.when(z == 2)
                def _():
                    far_hop(order[3], c, above, 0).start()
            multiply(plane, c, "first" if phase == 1 else "middle" if phase < PLANES else "last")
        if phase == 1:
            load_first.wait()
            load_second.wait()
        update(phase)

    for c in range(CHUNKS):
        for plane in range(PLANES):
            if c < HALF or plane in (0, 2):
                hop(order[plane], c, across, across_sem).wait_send()
            elif plane == 1:
                @pl.when(at_end)
                def _():
                    hop(order[plane], c, across, across_sem).wait_send()

            @pl.when(jnp.logical_and(has_above, plane <= z))
            def _():
                hop(plane, c, above, up_sem).wait_send()

            @pl.when(jnp.logical_and(has_below, plane >= z))
            def _():
                hop(plane, c, below, down_sem).wait_send()

        if c >= HALF:
            @pl.when(has_above)
            def _():
                far_hop(0, c, above, 0).wait_send()

            @pl.when(has_below)
            def _():
                far_hop(PLANES - 1, c, below, 1).wait_send()

    for g in range(BLOCKS):
        to_twin(g).wait_send()
    for i in range(BLOCKS - 1):
        to_peer(i).wait_send()

    @pl.when(core == 0)
    def _():
        to_peer(BLOCKS - 1).wait_send()


def finish_kernel(
    averaged, first_in, second_in, back, grad_acc, new_weights, new_first, new_second, input_grad,
    weights_out, first_out, second_out, pair_sem, back_sem, last_sem,
):
    order = plane_order(lax.div(lax.axis_index("tensor"), 2))
    depth, wide = grad_acc.shape
    rows_of = back.shape[0] // CHUNKS
    half = depth // 2

    def columns(plane):
        return pl.ds(pl.multiple_of(plane * wide, wide), wide)

    copies = []
    for i in range(PLANES - 1):
        at = columns(order[i])
        for k, (source, target) in enumerate(
            ((averaged, new_weights), (first_in, new_first), (second_in, new_second))
        ):
            copies.append(pltpu.make_async_copy(source.at[:, at], target.at[:, at], pair_sem.at[i, k]))
    for c in range(CHUNKS):
        part = pl.ds(c * rows_of, rows_of)
        copies.append(pltpu.make_async_copy(back.at[part], input_grad.at[part], back_sem.at[c]))
    for copy in copies:
        copy.start()
    at = columns(order[PLANES - 1])
    for h in range(2):
        @pl.loop(0, half // 128)
        def _(n):
            tile = pl.ds(pl.multiple_of(h * half + n * 128, 128), 128)
            weights_out[tile], first_out[tile], second_out[tile] = adam_tile(
                averaged[tile, at], grad_acc[tile], first_in[tile, at], second_in[tile, at]
            )

        part = pl.ds(h * half, half)
        for k, (source, target) in enumerate(
            ((weights_out, new_weights), (first_out, new_first), (second_out, new_second))
        ):
            copy = pltpu.make_async_copy(source.at[part], target.at[part, at], last_sem.at[h, k])
            copy.start()
            copies.append(copy)
    for copy in copies:
        copy.wait()


def on_device_fused(tokens, kv_grad, weights, first_moment, second_moment, exponent):
    tok, width, depth = tokens.shape[1], kv_grad.shape[2], weights.shape[1]
    bf16, f32 = jnp.bfloat16, jnp.float32
    wide = width * BLOCKS
    any_space = pl.BlockSpec(memory_space=pl.ANY)
    outs = pl.pallas_call(
        fused_kernel,
        out_shape=(
            pltpu.VMEM((depth, wide), f32),
            pltpu.VMEM((depth, wide), bf16),
            pltpu.VMEM((depth, wide), bf16),
            pltpu.VMEM((tok, depth), bf16),
            pltpu.VMEM((depth, 2 * width), f32),
        ),
        in_specs=[pl.BlockSpec(memory_space=pltpu.SMEM)] + [any_space] * 5,
        out_specs=[pl.BlockSpec(memory_space=pltpu.VMEM)] * 5,
        scratch_shapes=[
            pltpu.VMEM((BLOCKS, tok, width), bf16),
            pltpu.VMEM((tok, depth), bf16),
            pltpu.VMEM((depth, tok), bf16),
            pltpu.VMEM((BLOCKS, depth, width), bf16),
            pltpu.VMEM((BLOCKS, depth, width), bf16),
            pltpu.VMEM((BLOCKS, depth, width), bf16),
            pltpu.VMEM((BLOCKS, depth, width), bf16),
            pltpu.VMEM((tok, depth), f32),
            pltpu.SemaphoreType.DMA((PLANES, CHUNKS)),
            pltpu.SemaphoreType.DMA((PLANES, CHUNKS)),
            pltpu.SemaphoreType.DMA((PLANES, CHUNKS)),
            pltpu.SemaphoreType.DMA((2, CHUNKS)),
            pltpu.SemaphoreType.DMA((BLOCKS, CHUNKS)),
            pltpu.SemaphoreType.DMA((BLOCKS,)),
            pltpu.SemaphoreType.DMA((BLOCKS,)),
            pltpu.SemaphoreType.DMA((BLOCKS,)),
            pltpu.SemaphoreType.DMA((BLOCKS,)),
            pltpu.SemaphoreType.DMA,
            pltpu.SemaphoreType.DMA((BLOCKS,)),
            pltpu.SemaphoreType.DMA((CHUNKS,)),
            pltpu.SemaphoreType.DMA,
            pltpu.SemaphoreType.DMA,
        ],
        compiler_params=pltpu.CompilerParams(
            collective_id=0, has_side_effects=True, vmem_limit_bytes=46 << 20
        ),
    )(exponent, tokens[0], kv_grad[0], weights[0], first_moment[0], second_moment[0])
    results = pl.pallas_call(
        finish_kernel,
        out_shape=(
            jax.ShapeDtypeStruct((depth, wide), f32),
            jax.ShapeDtypeStruct((depth, wide), bf16),
            jax.ShapeDtypeStruct((depth, wide), bf16),
            jax.ShapeDtypeStruct((tok, depth), bf16),
        ),
        in_specs=[pl.BlockSpec(memory_space=pltpu.VMEM)] * 5,
        out_specs=[any_space] * 4,
        scratch_shapes=[
            pltpu.VMEM((depth, 2 * width), f32),
            pltpu.VMEM((depth, 2 * width), bf16),
            pltpu.VMEM((depth, 2 * width), bf16),
            pltpu.SemaphoreType.DMA((PLANES - 1, 3)),
            pltpu.SemaphoreType.DMA((CHUNKS,)),
            pltpu.SemaphoreType.DMA((2, 3)),
        ],
        compiler_params=pltpu.CompilerParams(vmem_limit_bytes=24 << 20),
    )(*outs)
    return tuple(out[None] for out in results)


def solution(mesh):
    small = mesh.shape["replica"] == 4 and mesh.shape["tensor"] == BLOCKS
    placed = (
        P("replica", None, "tensor"),
        P("replica", None, "tensor"),
        P("replica", "tensor", None),
        P("replica", "tensor", None),
        P("replica", "tensor", None),
        P(),
    )
    return jax.shard_map(
        on_device_fused if small else on_device,
        mesh=mesh,
        in_specs=placed,
        out_specs=(
            P("replica", "tensor", None),
            P("replica", "tensor", None),
            P("replica", "tensor", None),
            P("replica", None, "tensor"),
        ),
        check_vma=False,
    )
```
